256 devices in a mesh: col: 32 (over x, z_lo, core), row: 8 (over z_hi, y).
Axes of the slice: x: 4, y: 4, z: 8 (z_hi: 2, z_lo: 4; z = z_hi * 4 + z_lo), core: 2. Of those that a mesh axis runs over, the one named last changes fastest.
Arguments:
- objects: float32 [2, 2, 4096, 16384], P(None, None, 'row', 'col'), may hold values from -6 to 6
- probe: float32 [2, 256, 256], replicated, may hold values from -6 to 6
- measurements: float32 [8, 32, 3, 256, 256], P('row', 'col'), may hold values from 0.2 to 2.5
- offsets: int32 [8, 32, 3, 2], P('row', 'col'), may hold values from 0 to 512
- counts: int32 [8, 32], P('row', 'col'), may hold values from 1 to 3
Outputs:
- gradients: float32 [2, 2, 4096, 16384], P(None, None, 'row', 'col')
The draws below stay inside these ranges and needn't reach their ends.
Inputs may be any that keep to these rules, and one draw needn't show every extreme that they name: `offsets`: offsets place every window inside its tile with its border. Each tile uses its first counts positions.
All inputs are finite; a program needn't handle non-finite values.
Results may differ from the reference program's by a relative error of at most 0.0001.
Values sent between devices are 32-bit elements; how exact they have to be, the bound alone decides.
No kernel may reach another device: no remote copies, remote signals or barrier semaphores. Data moves between devices by JAX's collectives and lax.ppermute only.
A program may use at most 128 MiB of HBM per device.

```python
import jax
import jax.numpy as jnp
from jax import lax

SAMPLES = 2
POS = 3
PROBE = 256
TILE = 512
BORDER = 128
NTR = 8
NTC = 32
HEIGHT = 4096
WIDTH = 16384
REACH = 512


def set_ends(result, stream_key, low, largest):
    index_at = [jax.random.randint(jax.random.fold_in(stream_key, axis), (), 0, length) for axis, length in enumerate(result.shape)]
    main_axis = result.shape.index(max(result.shape))
    beside = index_at[:main_axis] + [(index_at[main_axis] + 1) % result.shape[main_axis]] + index_at[main_axis + 1:]
    return result.at[tuple(index_at)].set(low).at[tuple(beside)].set(largest)


def levels(own_key, dims, pieces, low, high):
    level, own = 1.0, jax.random.fold_in(own_key, 6)
    for dim, blocks in pieces:
        steps = jnp.exp(jax.random.uniform(jax.random.fold_in(own, dim), (blocks,), jnp.float32, low / len(pieces), high / len(pieces)))
        level = level * jnp.repeat(steps, dims[dim] // blocks).reshape([-1 if axis == dim else 1 for axis in range(len(dims))])
    return level


def bell_draw(rng, extent, deviation, most, split=(), kind=jnp.bfloat16):
    result = deviation * jax.random.normal(rng, extent, jnp.float32)
    if split:
        result = result * levels(rng, extent, split, -0.22, 0.18)
    return jnp.clip(result, -most, most).astype(kind)


def setup_inputs(seed: int = 0) -> dict:
    streams_of = jax.random.split(jax.random.key(seed), 6)
    return {
        "objects": bell_draw(streams_of[0], (SAMPLES, 2, HEIGHT, WIDTH), 0.7, 6.0, ((2, 8), (3, 32)), jnp.float32),
        "probe": bell_draw(streams_of[1], (2, PROBE, PROBE), 0.7, 6.0, (), jnp.float32),
        "measurements": jnp.clip(0.2 + 2.3 * jax.random.uniform(streams_of[2], (NTR, NTC, POS, PROBE, PROBE), jnp.float32) ** levels(streams_of[2], (NTR, NTC, POS, PROBE, PROBE), ((0, 8), (1, 32)), -0.2, 0.2), 0.2, 2.5),
        "offsets": set_ends(jax.random.randint(streams_of[3], (NTR, NTC, POS, 2), 0, REACH + 1), jax.random.fold_in(streams_of[3], 1), 0, REACH).astype(jnp.int32),
        "counts": set_ends(jax.random.randint(streams_of[4], (NTR, NTC), 1, POS + 1), jax.random.fold_in(streams_of[4], 1), 1, POS).astype(jnp.int32),
    }


smoothing = 0.5

def reference(objects, probe, measurements, offsets, counts):
    complex_obj = lax.complex(objects[:, 0], objects[:, 1])
    padded = jnp.pad(complex_obj, ((0, 0), (BORDER, BORDER), (BORDER, BORDER)))
    probe_wave = lax.complex(probe[0], probe[1])

    def visit(flat, gradient):
        flat = jnp.asarray(flat).astype(jnp.int32)
        tile_row = flat // (NTC * POS)
        tile_col = flat // POS % NTC
        position = flat % POS
        row_start = (tile_row * TILE + offsets[tile_row, tile_col, position, 0]).astype(jnp.int32)
        col_start = (tile_col * TILE + offsets[tile_row, tile_col, position, 1]).astype(jnp.int32)
        anchor = jnp.zeros((), jnp.int32)
        window = lax.dynamic_slice(padded, (anchor, row_start, col_start), (SAMPLES, PROBE, PROBE))
        spectrum = jnp.fft.fft2(probe_wave * window, norm='ortho')
        amplitude = jnp.sqrt(jnp.real(spectrum) * jnp.real(spectrum) + jnp.imag(spectrum) * jnp.imag(spectrum) + smoothing)
        factor = 1.0 - measurements[tile_row, tile_col, position] / amplitude
        back = jnp.fft.ifft2(spectrum * factor, norm='ortho')
        weight = (position < counts[tile_row, tile_col]).astype(amplitude.dtype)
        piece = jnp.conj(probe_wave) * back * weight
        current = lax.dynamic_slice(gradient, (anchor, row_start, col_start), (SAMPLES, PROBE, PROBE))
        return lax.dynamic_update_slice(gradient, current + piece, (anchor, row_start, col_start))
    gradient = lax.fori_loop(0, NTR * NTC * POS, visit, jnp.zeros_like(padded))
    inner = gradient[:, BORDER:BORDER + HEIGHT, BORDER:BORDER + WIDTH]
    return jnp.stack([jnp.real(inner), jnp.imag(inner)], axis=1)
```

```python
import functools
import math

import jax
import jax.numpy as jnp
import ml_dtypes
import numpy as np
from jax import lax
from jax.experimental import pallas as pl
from jax.experimental.pallas import tpu as pltpu
from jax.sharding import PartitionSpec as P

SAMPLES = 2
POS = 3
PROBE = 256
TILE = 512
BORDER = 128
EXT = TILE + 2 * BORDER
SMOOTHING = 0.5


def dft_tables():
    places = np.arange(PROBE, dtype=np.int64)
    angle = (places[:, None] * places[None, :] % PROBE) * (2.0 * math.pi / PROBE)
    scale = 1.0 / math.sqrt(PROBE)
    cosines, sines = np.cos(angle) * scale, np.sin(angle) * scale
    forward = np.block([[cosines, -sines], [sines, cosines]]).astype(np.float32)
    high = forward.astype(ml_dtypes.bfloat16)
    low = (forward - high.astype(np.float32)).astype(ml_dtypes.bfloat16)
    return np.stack([high, low, high.T, low.T])


def split(x):
    high = x.astype(jnp.bfloat16)
    low = (x - high.astype(jnp.float32)).astype(jnp.bfloat16)
    return high, low


def dot(a, b):
    return jnp.dot(a, b, preferred_element_type=jnp.float32)


def right_product(x, high, low):
    xh, xl = split(x)
    return dot(xh, high) + dot(xl, high) + dot(xh, low)


def left_product(high, low, x):
    xh, xl = split(x)
    return dot(high, xh) + dot(high, xl) + dot(low, xh)


PLACES = {
    "center": (BORDER, BORDER, TILE, TILE),
    "top": (0, BORDER, BORDER, TILE),
    "bottom": (BORDER + TILE, BORDER, BORDER, TILE),
    "left": (0, 0, EXT, BORDER),
    "right": (0, BORDER + TILE, EXT, BORDER),
}


def gradient_kernel(offsets, counts, *refs):
    names = list(PLACES)
    n = len(names)
    pieces = dict(zip(names, refs[:n]))
    probe, measurements, tables = refs[n : n + 3]
    outs = dict(zip(names, refs[n + 3 : 2 * n + 3]))
    obj, grad, sem = refs[2 * n + 3 :]
    samples = obj.shape[0]

    def view(ref, name):
        r, c, h, w = PLACES[name]
        return ref.at[:, :, pl.ds(r, h), pl.ds(c, w)]

    loads = [
        pltpu.make_async_copy(pieces[k], view(obj, k), sem.at[i])
        for i, k in enumerate(names)
    ]
    for copy in loads:
        copy.start()
    grad[...] = jnp.zeros_like(grad)
    for copy in loads:
        copy.wait()

    lanes = lax.broadcasted_iota(jnp.int32, (PROBE, 128), 1)
    rows = lax.broadcasted_iota(jnp.int32, (8, 128), 0)

    def visit(q, carry):
        r0 = offsets[q * 2]
        c0 = offsets[q * 2 + 1]
        rt, ct = lax.rem(r0, 8), lax.rem(c0, 128)
        ra = pl.multiple_of(r0 - rt, 8)
        rz = pl.multiple_of(jnp.minimum(ra + PROBE, EXT - 8), 8)
        ca = pl.multiple_of(c0 - ct, 128)
        cb = pl.multiple_of(ca + 128, 128)
        cz = pl.multiple_of(jnp.minimum(ca + 256, EXT - 128), 128)
        early = lanes < ct
        above = rows < rt

        pr = pltpu.roll(pltpu.roll(probe[0], rt, 0), ct, 1)
        pi = pltpu.roll(pltpu.roll(probe[1], rt, 0), ct, 1)

        def block(s, k, col):
            head = jnp.where(
                above,
                obj[s, k, pl.ds(rz, 8), pl.ds(col, 128)],
                obj[s, k, pl.ds(ra, 8), pl.ds(col, 128)],
            )
            tail = obj[s, k, pl.ds(pl.multiple_of(ra + 8, 8), PROBE - 8), pl.ds(col, 128)]
            return jnp.concatenate([head, tail], axis=0)

        def frame(s, k):
            first = jnp.where(early, block(s, k, cz), block(s, k, ca))
            return jnp.concatenate([first, block(s, k, cb)], axis=1)

        def scatter(s, k, value):
            def add(col, v):
                grad[s, k, pl.ds(pl.multiple_of(ra + 8, 8), PROBE - 8), pl.ds(col, 128)] += v[8:]
                grad[s, k, pl.ds(ra, 8), pl.ds(col, 128)] += jnp.where(above, 0.0, v[:8])
                grad[s, k, pl.ds(rz, 8), pl.ds(col, 128)] += jnp.where(above, v[:8], 0.0)

            first = value[:, :128]
            add(ca, jnp.where(early, 0.0, first))
            add(cz, jnp.where(early, first, 0.0))
            add(cb, value[:, 128:])

        stacked = []
        for s in range(samples):
            o_r, o_i = frame(s, 0), frame(s, 1)
            stacked.append(
                jnp.concatenate([pr * o_r - pi * o_i, pr * o_i + pi * o_r], axis=1)
            )
        wave = jnp.concatenate(stacked, axis=0)
        half = right_product(wave, tables[0], tables[1])
        turned = jnp.concatenate(
            [
                jnp.concatenate(
                    [half[s * PROBE : (s + 1) * PROBE, k * PROBE : (k + 1) * PROBE] for s in range(samples)],
                    axis=1,
                )
                for k in range(2)
            ],
            axis=0,
        )
        spectrum = left_product(tables[2], tables[3], turned)
        s_r, s_i = spectrum[:PROBE], spectrum[PROBE:]
        m = measurements[q]
        m = jnp.concatenate([m] * samples, axis=1)
        factor = 1.0 - m * lax.rsqrt(s_r * s_r + s_i * s_i + SMOOTHING)
        scaled = jnp.concatenate([s_r * factor, s_i * factor], axis=0)
        back = left_product(tables[0], tables[1], scaled)
        back = jnp.concatenate(
            [
                jnp.concatenate(
                    [back[:PROBE, s * PROBE : (s + 1) * PROBE], back[PROBE:, s * PROBE : (s + 1) * PROBE]],
                    axis=1,
                )
                for s in range(samples)
            ],
            axis=0,
        )
        final = right_product(back, tables[2], tables[3])
        for s in range(samples):
            b_r = final[s * PROBE : (s + 1) * PROBE, :PROBE]
            b_i = final[s * PROBE : (s + 1) * PROBE, PROBE:]
            scatter(s, 0, pr * b_r + pi * b_i)
            scatter(s, 1, pr * b_i - pi * b_r)
        return carry

    lax.fori_loop(0, counts[0], visit, 0)
    stores = [
        pltpu.make_async_copy(view(grad, k), outs[k], sem.at[i])
        for i, k in enumerate(names)
    ]
    for copy in stores:
        copy.start()
    for copy in stores:
        copy.wait()


def window_gradients(pieces, probe, measurements, offsets, counts):
    samples = pieces["center"].shape[0]
    names = list(PLACES)
    shapes = [jax.ShapeDtypeStruct((samples, 2) + PLACES[k][2:], jnp.float32) for k in names]
    anywhere = pl.BlockSpec(memory_space=pl.ANY)
    inside = pl.BlockSpec(memory_space=pltpu.VMEM)
    scalars = pl.BlockSpec(memory_space=pltpu.SMEM)
    outs = pl.pallas_call(
        gradient_kernel,
        out_shape=shapes,
        in_specs=[scalars, scalars] + [anywhere] * len(names) + [inside] * 3,
        out_specs=[anywhere] * len(names),
        scratch_shapes=[
            pltpu.VMEM((samples, 2, EXT, EXT), jnp.float32),
            pltpu.VMEM((samples, 2, EXT, EXT), jnp.float32),
            pltpu.SemaphoreType.DMA((len(names),)),
        ],
        compiler_params=pltpu.CompilerParams(vmem_limit_bytes=56 * 1024 * 1024),
    )(
        offsets.reshape(-1),
        counts.reshape(-1),
        *[pieces[k] for k in names],
        probe,
        measurements,
        jnp.asarray(dft_tables()),
    )
    return dict(zip(names, outs))


def shifted(x, axis, by):
    count = lax.axis_size(axis)
    pairs = [(i, i + by) for i in range(count) if 0 <= i + by < count]
    return lax.ppermute(x, axis, pairs)


def body(objects, probe, measurements, offsets, counts):
    top = shifted(objects[:, :, TILE - BORDER :, :], "row", 1)
    bottom = shifted(objects[:, :, :BORDER, :], "row", -1)

    def column(lo):
        return jnp.concatenate([x[..., lo : lo + BORDER] for x in (top, objects, bottom)], axis=2)

    left = shifted(column(TILE - BORDER), "col", 1)
    right = shifted(column(0), "col", -1)
    pieces = dict(center=objects, top=top, bottom=bottom, left=left, right=right)
    g = window_gradients(pieces, probe, measurements[0, 0], offsets, counts)
    from_right = shifted(g["left"], "col", -1)
    from_left = shifted(g["right"], "col", 1)

    def folded(x, lo, hi):
        x = x.at[..., TILE - BORDER :].add(from_right[:, :, lo:hi])
        return x.at[..., :BORDER].add(from_left[:, :, lo:hi])

    from_below = shifted(folded(g["top"], 0, BORDER), "row", -1)
    from_above = shifted(folded(g["bottom"], BORDER + TILE, EXT), "row", 1)
    result = folded(g["center"], BORDER, BORDER + TILE)
    result = result.at[:, :, TILE - BORDER :].add(from_below)
    return result.at[:, :, :BORDER].add(from_above)


def solution(mesh):
    in_specs = (
        P(None, None, "row", "col"),
        P(),
        P("row", "col", None, None, None),
        P("row", "col", None, None),
        P("row", "col"),
    )
    out_specs = P(None, None, "row", "col")
    return jax.shard_map(body, mesh=mesh, in_specs=in_specs, out_specs=out_specs, check_vma=False)
```

```python
import functools
import math

import jax
import jax.numpy as jnp
import ml_dtypes
import numpy as np
from jax import lax
from jax.experimental import pallas as pl
from jax.experimental.pallas import tpu as pltpu
from jax.sharding import PartitionSpec as P

SAMPLES = 2
POS = 3
PROBE = 256
TILE = 512
BORDER = 128
EXT = TILE + 2 * BORDER
SMOOTHING = 0.5


def dft_tables():
    places = np.arange(PROBE, dtype=np.int64)
    angle = (places[:, None] * places[None, :] % PROBE) * (2.0 * math.pi / PROBE)
    scale = 1.0 / math.sqrt(PROBE)
    cosines, sines = np.cos(angle) * scale, np.sin(angle) * scale
    forward = np.block([[cosines, -sines], [sines, cosines]]).astype(np.float32)
    high = forward.astype(ml_dtypes.bfloat16)
    low = (forward - high.astype(np.float32)).astype(ml_dtypes.bfloat16)
    return np.stack([high, low, high.T, low.T])


def split(x):
    high = x.astype(jnp.bfloat16)
    low = (x - high.astype(jnp.float32)).astype(jnp.bfloat16)
    return high, low


def dot(a, b):
    return jnp.dot(a, b, preferred_element_type=jnp.float32)


def right_product(x, high, low):
    xh, xl = split(x)
    return dot(xh, high) + dot(xl, high) + dot(xh, low)


def left_product(high, low, x):
    xh, xl = split(x)
    return dot(high, xh) + dot(high, xl) + dot(low, xh)


PLACES = {
    "center": (BORDER, BORDER, TILE, TILE),
    "top": (0, BORDER, BORDER, TILE),
    "bottom": (BORDER + TILE, BORDER, BORDER, TILE),
    "left": (0, 0, EXT, BORDER),
    "right": (0, BORDER + TILE, EXT, BORDER),
}


def gradient_kernel(sample, offsets, counts, *refs):
    names = list(PLACES)
    n = len(names)
    pieces = dict(zip(names, refs[:n]))
    fixed = refs[n : n + 3]
    outs = dict(zip(names, refs[n + 3 : 2 * n + 3]))
    obj, grad, probe, measurements, tables, sem = refs[2 * n + 3 :]
    samples = obj.shape[0]

    def view(ref, name):
        r, c, h, w = PLACES[name]
        return ref.at[:, :, pl.ds(r, h), pl.ds(c, w)]

    loads = [
        pltpu.make_async_copy(
            pieces[k].at[pl.ds(sample, 1)] if k == "center" else pieces[k], view(obj, k), sem.at[i]
        )
        for i, k in enumerate(names)
    ]
    loads += [
        pltpu.make_async_copy(src, dst, sem.at[n + i])
        for i, (src, dst) in enumerate(zip(fixed, (probe, measurements, tables)))
    ]
    for copy in loads:
        copy.start()
    grad[...] = jnp.zeros_like(grad)
    for copy in loads:
        copy.wait()

    lanes = lax.broadcasted_iota(jnp.int32, (PROBE, 128), 1)
    rows = lax.broadcasted_iota(jnp.int32, (8, 128), 0)

    def visit(q, carry):
        r0 = offsets[q * 2]
        c0 = offsets[q * 2 + 1]
        rt, ct = lax.rem(r0, 8), lax.rem(c0, 128)
        ra = pl.multiple_of(r0 - rt, 8)
        rz = pl.multiple_of(jnp.minimum(ra + PROBE, EXT - 8), 8)
        ca = pl.multiple_of(c0 - ct, 128)
        cb = pl.multiple_of(ca + 128, 128)
        cz = pl.multiple_of(jnp.minimum(ca + 256, EXT - 128), 128)
        early = lanes < ct
        above = rows < rt

        pr = pltpu.roll(pltpu.roll(probe[0], rt, 0), ct, 1)
        pi = pltpu.roll(pltpu.roll(probe[1], rt, 0), ct, 1)

        def block(s, k, col):
            head = jnp.where(
                above,
                obj[s, k, pl.ds(rz, 8), pl.ds(col, 128)],
                obj[s, k, pl.ds(ra, 8), pl.ds(col, 128)],
            )
            tail = obj[s, k, pl.ds(pl.multiple_of(ra + 8, 8), PROBE - 8), pl.ds(col, 128)]
            return jnp.concatenate([head, tail], axis=0)

        def frame(s, k):
            first = jnp.where(early, block(s, k, cz), block(s, k, ca))
            return jnp.concatenate([first, block(s, k, cb)], axis=1)

        def scatter(s, k, value):
            def add(col, v):
                grad[s, k, pl.ds(pl.multiple_of(ra + 8, 8), PROBE - 8), pl.ds(col, 128)] += v[8:]
                grad[s, k, pl.ds(ra, 8), pl.ds(col, 128)] += jnp.where(above, 0.0, v[:8])
                grad[s, k, pl.ds(rz, 8), pl.ds(col, 128)] += jnp.where(above, v[:8], 0.0)

            first = value[:, :128]
            add(ca, jnp.where(early, 0.0, first))
            add(cz, jnp.where(early, first, 0.0))
            add(cb, value[:, 128:])

        stacked = []
        for s in range(samples):
            o_r, o_i = frame(s, 0), frame(s, 1)
            stacked.append(
                jnp.concatenate([pr * o_r - pi * o_i, pr * o_i + pi * o_r], axis=1)
            )
        wave = jnp.concatenate(stacked, axis=0)
        half = right_product(wave, tables[0], tables[1])
        turned = jnp.concatenate(
            [
                jnp.concatenate(
                    [half[s * PROBE : (s + 1) * PROBE, k * PROBE : (k + 1) * PROBE] for s in range(samples)],
                    axis=1,
                )
                for k in range(2)
            ],
            axis=0,
        )
        spectrum = left_product(tables[2], tables[3], turned)
        s_r, s_i = spectrum[:PROBE], spectrum[PROBE:]
        m = measurements[q]
        m = jnp.concatenate([m] * samples, axis=1)
        factor = 1.0 - m * lax.rsqrt(s_r * s_r + s_i * s_i + SMOOTHING)
        scaled = jnp.concatenate([s_r * factor, s_i * factor], axis=0)
        back = left_product(tables[0], tables[1], scaled)
        back = jnp.concatenate(
            [
                jnp.concatenate(
                    [back[:PROBE, s * PROBE : (s + 1) * PROBE], back[PROBE:, s * PROBE : (s + 1) * PROBE]],
                    axis=1,
                )
                for s in range(samples)
            ],
            axis=0,
        )
        final = right_product(back, tables[2], tables[3])
        for s in range(samples):
            b_r = final[s * PROBE : (s + 1) * PROBE, :PROBE]
            b_i = final[s * PROBE : (s + 1) * PROBE, PROBE:]
            scatter(s, 0, pr * b_r + pi * b_i)
            scatter(s, 1, pr * b_i - pi * b_r)
        return carry

    lax.fori_loop(0, counts[0], visit, 0)
    stores = [
        pltpu.make_async_copy(view(grad, k), outs[k], sem.at[i])
        for i, k in enumerate(names)
    ]
    for copy in stores:
        copy.start()
    for copy in stores:
        copy.wait()


def window_gradients(sample, pieces, probe, measurements, offsets, counts, tables):
    names = list(PLACES)
    shapes = [jax.ShapeDtypeStruct((1, 2) + PLACES[k][2:], jnp.float32) for k in names]
    anywhere = pl.BlockSpec(memory_space=pl.ANY)
    scalars = pl.BlockSpec(memory_space=pltpu.SMEM)
    outs = pl.pallas_call(
        functools.partial(gradient_kernel, sample),
        out_shape=shapes,
        in_specs=[scalars, scalars] + [anywhere] * (len(names) + 3),
        out_specs=[pl.BlockSpec(memory_space=pltpu.HBM)] + [anywhere] * (len(names) - 1),
        scratch_shapes=[
            pltpu.VMEM((1, 2, EXT, EXT), jnp.float32),
            pltpu.VMEM((1, 2, EXT, EXT), jnp.float32),
            pltpu.VMEM((2, PROBE, PROBE), jnp.float32),
            pltpu.VMEM((POS, PROBE, PROBE), jnp.float32),
            pltpu.VMEM((4, 2 * PROBE, 2 * PROBE), jnp.bfloat16),
            pltpu.SemaphoreType.DMA((len(names) + 3,)),
        ],
        compiler_params=pltpu.CompilerParams(vmem_limit_bytes=40 * 1024 * 1024),
        cost_estimate=pl.CostEstimate(flops=10**10, bytes_accessed=3 * 10**7, transcendentals=0),
    )(
        offsets.reshape(-1),
        counts.reshape(-1),
        *[pieces[k] for k in names],
        probe,
        measurements,
        tables,
    )
    return dict(zip(names, outs))


def side_kernel(center, from_left, from_right, *refs):
    out = refs[-1]
    out[0, 0] = center[0, 0]
    out[0, 0, :, :BORDER] += from_left[0, 0]
    out[0, 0, :, TILE - BORDER :] += from_right[0, 0]


def add_sides(sample, center, from_left, from_right, into=None):
    part = BORDER

    def block(width, first):
        return pl.BlockSpec((1, 1, part, width), lambda k, i: (0, k, i + first, 0))

    args = [center, from_left, from_right]
    specs = [block(TILE, 0), block(BORDER, 1), block(BORDER, 1)]
    aliases = {}
    if into is not None:
        aliases = {len(args): 0}
        args.append(into)
        specs.append(pl.BlockSpec(memory_space=pl.ANY))
    return pl.pallas_call(
        side_kernel,
        out_shape=jax.ShapeDtypeStruct((SAMPLES, 2, TILE, TILE), jnp.float32),
        grid=(2, TILE // part),
        in_specs=specs,
        out_specs=pl.BlockSpec((1, 1, part, TILE), lambda k, i: (sample, k, i, 0)),
        input_output_aliases=aliases,
        cost_estimate=pl.CostEstimate(flops=10**6, bytes_accessed=6 * 10**6, transcendentals=0),
    )(*args)


def edge_kernel(place, above0, below0, crossed0, above1, below1, held, out, band, got, sem):
    row, last = place[0], place[1]
    far = TILE - BORDER
    loads = []
    for s in range(SAMPLES):
        for e, first in enumerate((0, far)):
            loads.append((out.at[s, :, pl.ds(first, BORDER)], band.at[s, e]))
    strips = (above0.at[0], below0.at[0], above1.at[0], below1.at[0], crossed0.at[0])
    loads += [(src, got.at[i]) for i, src in enumerate(strips)]
    loads = [pltpu.make_async_copy(a, b, sem.at[i]) for i, (a, b) in enumerate(loads)]
    for copy in loads:
        copy.start()
    for copy in loads:
        copy.wait()
    band[0, 0] += jnp.where(row == TURN, got[4], jnp.where(row == 0, 0.0, got[0]))
    band[0, 1] += jnp.where(row == TURN - 1, got[4], jnp.where(row == last, 0.0, got[1]))
    band[1, 0] += got[2]
    band[1, 1] += got[3]
    stores = []
    for s in range(SAMPLES):
        for e, first in enumerate((0, far)):
            i = len(stores)
            stores.append(
                pltpu.make_async_copy(band.at[s, e], out.at[s, :, pl.ds(first, BORDER)], sem.at[i])
            )
    for copy in stores:
        copy.start()
    for copy in stores:
        copy.wait()


def add_edges(place, out, above0, below0, crossed0, above1, below1):
    anywhere = pl.BlockSpec(memory_space=pl.ANY)
    return pl.pallas_call(
        edge_kernel,
        out_shape=jax.ShapeDtypeStruct(out.shape, out.dtype),
        in_specs=[pl.BlockSpec(memory_space=pltpu.SMEM)] + [anywhere] * 6,
        out_specs=anywhere,
        scratch_shapes=[
            pltpu.VMEM((SAMPLES, 2, 2, BORDER, TILE), jnp.float32),
            pltpu.VMEM((5, 2, BORDER, TILE), jnp.float32),
            pltpu.SemaphoreType.DMA((9,)),
        ],
        input_output_aliases={6: 0},
        cost_estimate=pl.CostEstimate(flops=10**6, bytes_accessed=6 * 10**6, transcendentals=0),
    )(place, above0, below0, crossed0, above1, below1, out)


TURN = 4


def moved(x, axis, pairs):
    return lax.ppermute(x, axis, pairs)


def steps(axis, by):
    count = lax.axis_size(axis)
    return [(i, i + by) for i in range(count) if 0 <= i + by < count]


def detours():
    last = lax.axis_size("row") - 1
    down = [p for p in steps("row", 1) if p != (TURN - 1, TURN)] + [(TURN - 1, 0)]
    up = [p for p in steps("row", -1) if p != (TURN, TURN - 1)] + [(TURN, last)]
    return down, up, [(0, TURN), (last, TURN - 1)]


def body(objects, probe, measurements, offsets, counts):
    row = lax.axis_index("row")
    rows = lax.axis_size("row")
    last = rows - 1
    place = jnp.stack([row, jnp.int32(last)]).astype(jnp.int32)
    down, up, over = detours()
    tables = jnp.asarray(dft_tables())
    args = (probe, measurements[0, 0], offsets, counts, tables)

    low, high = objects[:, :, TILE - BORDER :], objects[:, :, :BORDER]
    top1 = moved(low[1:], "row", down)
    bottom1 = moved(high[1:], "row", up)
    top0 = moved(low[:1], "row", steps("row", 1))
    bottom0 = moved(high[:1], "row", steps("row", -1))
    crossed1 = moved(jnp.where(row == 0, top1, bottom1), "row", over)
    top1 = jnp.where(row == TURN, crossed1, jnp.where(row == 0, 0.0, top1))
    bottom1 = jnp.where(row == TURN - 1, crossed1, jnp.where(row == last, 0.0, bottom1))

    def sides(s, top, bottom):
        def column(lo):
            return jnp.concatenate(
                [x[..., lo : lo + BORDER] for x in (top, objects[s : s + 1], bottom)], axis=2
            )

        left = moved(column(TILE - BORDER), "col", steps("col", 1))
        right = moved(column(0), "col", steps("col", -1))
        return dict(center=objects, top=top, bottom=bottom, left=left, right=right)

    pieces0, pieces1 = lax.optimization_barrier(
        (sides(0, top0, bottom0), sides(1, top1, bottom1))
    )
    g0 = window_gradients(0, pieces0, *args)
    g1 = window_gradients(1, pieces1, *args)

    def fold(g):
        from_right = moved(g["left"], "col", steps("col", -1))
        from_left = moved(g["right"], "col", steps("col", 1))

        def folded(x, lo):
            x = x.at[..., TILE - BORDER :].add(from_right[:, :, lo : lo + BORDER])
            return x.at[..., :BORDER].add(from_left[:, :, lo : lo + BORDER])

        return from_left, from_right, folded(g["top"], 0), folded(g["bottom"], BORDER + TILE)

    left0, right0, first0, final0 = fold(g0)
    above0 = moved(final0, "row", down)
    below0 = moved(first0, "row", up)
    crossed0 = moved(jnp.where(row == 0, above0, below0), "row", over)
    left1, right1, first1, final1 = fold(g1)
    above1 = moved(final1, "row", steps("row", 1))
    below1 = moved(first1, "row", steps("row", -1))
    out = add_sides(0, g0["center"], left0, right0)
    out = add_sides(1, g1["center"], left1, right1, into=out)
    return add_edges(place, out, above0, below0, crossed0, above1, below1)


def solution(mesh):
    in_specs = (
        P(None, None, "row", "col"),
        P(),
        P("row", "col", None, None, None),
        P("row", "col", None, None),
        P("row", "col"),
    )
    out_specs = P(None, None, "row", "col")
    return jax.shard_map(body, mesh=mesh, in_specs=in_specs, out_specs=out_specs, check_vma=False)
```

```python
import functools
import math

import jax
import jax.numpy as jnp
import ml_dtypes
import numpy as np
from jax import lax
from jax.experimental import pallas as pl
from jax.experimental.pallas import tpu as pltpu
from jax.sharding import PartitionSpec as P

SAMPLES = 2
POS = 3
PROBE = 256
TILE = 512
BORDER = 128
EXT = TILE + 2 * BORDER
SMOOTHING = 0.5


def dft_tables():
    places = np.arange(PROBE, dtype=np.int64)
    angle = (places[:, None] * places[None, :] % PROBE) * (2.0 * math.pi / PROBE)
    scale = 1.0 / math.sqrt(PROBE)
    cosines, sines = np.cos(angle) * scale, np.sin(angle) * scale
    forward = np.block([[cosines, -sines], [sines, cosines]]).astype(np.float32)
    high = forward.astype(ml_dtypes.bfloat16)
    low = (forward - high.astype(np.float32)).astype(ml_dtypes.bfloat16)
    return np.stack([high, low, high.T, low.T])


def split(x):
    high = x.astype(jnp.bfloat16)
    low = (x - high.astype(jnp.float32)).astype(jnp.bfloat16)
    return high, low


def dot(a, b):
    return jnp.dot(a, b, preferred_element_type=jnp.float32)


def right_product(x, high, low):
    xh, xl = split(x)
    return dot(xh, high) + dot(xl, high) + dot(xh, low)


def left_product(high, low, x):
    xh, xl = split(x)
    return dot(high, xh) + dot(high, xl) + dot(low, xh)


FAR = BORDER + TILE
TURN = 4


def spots(place, far):
    row_a = jnp.where(lax.rem(place[0], 2) == 0, far, 0)
    col_a = jnp.where(place[2] == 0, far, 0)
    return [pl.multiple_of(v, BORDER) for v in (row_a, far - row_a, col_a, far - col_a)]


def regions(place):
    ra, rb, ca, cb = spots(place, FAR)
    return [
        (0, SAMPLES, BORDER, TILE, BORDER, TILE),
        (0, SAMPLES, ra, BORDER, BORDER, TILE),
        (0, 1, rb, BORDER, BORDER, TILE),
        (1, 1, rb, BORDER, BORDER, TILE),
        (0, SAMPLES, BORDER, TILE, ca, BORDER),
        (0, SAMPLES, BORDER, TILE, cb, BORDER),
        (0, SAMPLES, ra, BORDER, ca, BORDER),
        (0, SAMPLES, rb, BORDER, ca, BORDER),
        (0, SAMPLES, ra, BORDER, cb, BORDER),
        (0, SAMPLES, rb, BORDER, cb, BORDER),
    ]


def region_of(array, region):
    s, n, r, h, c, w = region
    return array.at[pl.ds(s, n), :, pl.ds(r, h), pl.ds(c, w)]


def halves(ref):
    return [ref.at[:, :, pl.ds(h * BORDER, BORDER)] for h in range(2)]


def turns(place):
    row = place[0]
    return (row == TURN) | (row == TURN - 1), (row == 0) | (row == place[1])


def load_pieces(place, obj, refs, sem):
    center, strip_a, strip_b0, strip_b1, crossed, side_a, side_b, end_a, end_b = refs
    sources = [center, strip_a, strip_b0, strip_b1, side_a, side_b] + halves(end_a) + halves(end_b)
    at_turn, at_end = turns(place)
    where = regions(place)
    copies = [
        pltpu.make_async_copy(src, region_of(obj, region), sem.at[i])
        for i, (src, region) in enumerate(zip(sources, where))
    ]
    for i, copy in enumerate(copies):
        if i != 3:
            copy.start()
    relayed = pltpu.make_async_copy(crossed, region_of(obj, where[3]), sem.at[3])

    @pl.when(at_turn)
    def _():
        relayed.start()

    @pl.when(jnp.logical_not(at_turn))
    def _():
        copies[3].start()

    def wait():
        for copy in copies:
            copy.wait()

        @pl.when(at_end)
        def _():
            region_of(obj, where[3])[...] = jnp.zeros((1, 2, BORDER, TILE), jnp.float32)

    return wait


def store_pieces(place, grad, refs, sem):
    center, strip_a, strip_b0, strip_b1, side_a, side_b, end_a, end_b = refs
    targets = [center, strip_a, strip_b0, strip_b1, side_a, side_b] + halves(end_a) + halves(end_b)
    copies = [
        pltpu.make_async_copy(region_of(grad, region), dst, sem.at[i])
        for i, (dst, region) in enumerate(zip(targets, regions(place)))
    ]
    for copy in copies[::-1]:
        copy.start()
    for copy in copies:
        copy.wait()


def gradient_kernel(place, offsets, counts, *refs):
    ins, fixed, outs = refs[:9], refs[9:12], refs[12:20]
    obj, grad, probe, measurements, tables, sem = refs[20:]
    samples = SAMPLES
    fixed_loads = [
        pltpu.make_async_copy(src, dst, sem.at[16 + i])
        for i, (src, dst) in enumerate(zip(fixed, (probe, measurements, tables)))
    ]
    for copy in fixed_loads:
        copy.start()
    wait = load_pieces(place, obj, ins, sem)
    grad[...] = jnp.zeros_like(grad)
    for copy in fixed_loads:
        copy.wait()
    wait()

    lanes = lax.broadcasted_iota(jnp.int32, (PROBE, 128), 1)
    rows = lax.broadcasted_iota(jnp.int32, (8, 128), 0)

    def visit(q, carry):
        r0 = offsets[q * 2]
        c0 = offsets[q * 2 + 1]
        rt, ct = lax.rem(r0, 8), lax.rem(c0, 128)
        ra = pl.multiple_of(r0 - rt, 8)
        rz = pl.multiple_of(jnp.minimum(ra + PROBE, EXT - 8), 8)
        ca = pl.multiple_of(c0 - ct, 128)
        cb = pl.multiple_of(ca + 128, 128)
        cz = pl.multiple_of(jnp.minimum(ca + 256, EXT - 128), 128)
        early = lanes < ct
        above = rows < rt

        pr = pltpu.roll(pltpu.roll(probe[0], rt, 0), ct, 1)
        pi = pltpu.roll(pltpu.roll(probe[1], rt, 0), ct, 1)

        def block(s, k, col):
            head = jnp.where(
                above,
                obj[s, k, pl.ds(rz, 8), pl.ds(col, 128)],
                obj[s, k, pl.ds(ra, 8), pl.ds(col, 128)],
            )
            tail = obj[s, k, pl.ds(pl.multiple_of(ra + 8, 8), PROBE - 8), pl.ds(col, 128)]
            return jnp.concatenate([head, tail], axis=0)

        def frame(s, k):
            first = jnp.where(early, block(s, k, cz), block(s, k, ca))
            return jnp.concatenate([first, block(s, k, cb)], axis=1)

        def scatter(s, k, value):
            def add(col, v):
                grad[s, k, pl.ds(pl.multiple_of(ra + 8, 8), PROBE - 8), pl.ds(col, 128)] += v[8:]
                grad[s, k, pl.ds(ra, 8), pl.ds(col, 128)] += jnp.where(above, 0.0, v[:8])
                grad[s, k, pl.ds(rz, 8), pl.ds(col, 128)] += jnp.where(above, v[:8], 0.0)

            first = value[:, :128]
            add(ca, jnp.where(early, 0.0, first))
            add(cz, jnp.where(early, first, 0.0))
            add(cb, value[:, 128:])

        stacked = []
        for s in range(samples):
            o_r, o_i = frame(s, 0), frame(s, 1)
            stacked.append(
                jnp.concatenate([pr * o_r - pi * o_i, pr * o_i + pi * o_r], axis=1)
            )
        wave = jnp.concatenate(stacked, axis=0)
        half = right_product(wave, tables[0], tables[1])
        turned = jnp.concatenate(
            [
                jnp.concatenate(
                    [half[s * PROBE : (s + 1) * PROBE, k * PROBE : (k + 1) * PROBE] for s in range(samples)],
                    axis=1,
                )
                for k in range(2)
            ],
            axis=0,
        )
        spectrum = left_product(tables[2], tables[3], turned)
        s_r, s_i = spectrum[:PROBE], spectrum[PROBE:]
        m = measurements[q]
        m = jnp.concatenate([m] * samples, axis=1)
        factor = 1.0 - m * lax.rsqrt(s_r * s_r + s_i * s_i + SMOOTHING)
        scaled = jnp.concatenate([s_r * factor, s_i * factor], axis=0)
        back = left_product(tables[0], tables[1], scaled)
        back = jnp.concatenate(
            [
                jnp.concatenate(
                    [back[:PROBE, s * PROBE : (s + 1) * PROBE], back[PROBE:, s * PROBE : (s + 1) * PROBE]],
                    axis=1,
                )
                for s in range(samples)
            ],
            axis=0,
        )
        final = right_product(back, tables[2], tables[3])
        for s in range(samples):
            b_r = final[s * PROBE : (s + 1) * PROBE, :PROBE]
            b_i = final[s * PROBE : (s + 1) * PROBE, PROBE:]
            scatter(s, 0, pr * b_r + pi * b_i)
            scatter(s, 1, pr * b_i - pi * b_r)
        return carry

    lax.fori_loop(0, counts[0], visit, 0)
    store_pieces(place, grad, outs, sem)


def window_gradients(place, pieces, probe, measurements, offsets, counts, tables):
    def shape(*dims):
        return jax.ShapeDtypeStruct(dims, jnp.float32)

    strip, side = shape(1, 2, BORDER, TILE), shape(SAMPLES, 2, TILE, BORDER)
    end = shape(SAMPLES, 2, 2 * BORDER, BORDER)
    shapes = [shape(SAMPLES, 2, TILE, TILE), shape(SAMPLES, 2, BORDER, TILE)]
    shapes += [strip] * 2 + [side] * 2 + [end] * 2
    anywhere = pl.BlockSpec(memory_space=pl.ANY)
    scalars = pl.BlockSpec(memory_space=pltpu.SMEM)
    return pl.pallas_call(
        gradient_kernel,
        out_shape=shapes,
        in_specs=[scalars] * 3 + [anywhere] * (len(pieces) + 3),
        out_specs=[pl.BlockSpec(memory_space=pltpu.HBM)] + [anywhere] * 7,
        scratch_shapes=[
            pltpu.VMEM((SAMPLES, 2, EXT, EXT), jnp.float32),
            pltpu.VMEM((SAMPLES, 2, EXT, EXT), jnp.float32),
            pltpu.VMEM((2, PROBE, PROBE), jnp.float32),
            pltpu.VMEM((POS, PROBE, PROBE), jnp.float32),
            pltpu.VMEM((4, 2 * PROBE, 2 * PROBE), jnp.bfloat16),
            pltpu.SemaphoreType.DMA((20,)),
        ],
        compiler_params=pltpu.CompilerParams(vmem_limit_bytes=48 * 1024 * 1024),
        cost_estimate=pl.CostEstimate(flops=10**10, bytes_accessed=3 * 10**7, transcendentals=0),
    )(place, offsets.reshape(-1), counts.reshape(-1), *pieces, probe, measurements, tables)


def side_kernel(place, side_a, side_b, held, out, band, got, sem):
    starts = spots(place, TILE - BORDER)[2:]
    loads = []
    for e, (src, first) in enumerate(zip((side_a, side_b), starts)):
        loads.append((out.at[:, :, :, pl.ds(first, BORDER)], band.at[e]))
        loads.append((src, got.at[e]))
    loads = [pltpu.make_async_copy(a, b, sem.at[i]) for i, (a, b) in enumerate(loads)]
    for copy in loads:
        copy.start()
    for copy in loads:
        copy.wait()
    band[...] += got[...]
    stores = [
        pltpu.make_async_copy(band.at[e], out.at[:, :, :, pl.ds(first, BORDER)], sem.at[e])
        for e, first in enumerate(starts)
    ]
    for copy in stores:
        copy.start()
    for copy in stores:
        copy.wait()


def edge_kernel(place, strip_a, strip_b0, strip_b1, crossed, held, out, band, got, sem):
    starts = spots(place, TILE - BORDER)[:2]
    at_turn, at_end = turns(place)
    bands = [
        (out.at[s, :, pl.ds(first, BORDER)], band.at[e, s])
        for e, first in enumerate(starts)
        for s in range(SAMPLES)
    ]
    strips = (strip_a.at[0], strip_a.at[1], strip_b0.at[0], strip_b1.at[0], crossed.at[0])
    loads = bands + [(src, got.at[i]) for i, src in enumerate(strips)]
    loads = [pltpu.make_async_copy(a, b, sem.at[i]) for i, (a, b) in enumerate(loads)]
    for copy in loads:
        copy.start()
    for copy in loads:
        copy.wait()
    band[0, 0] += got[0]
    band[0, 1] += got[1]
    band[1, 0] += got[2]
    band[1, 1] += jnp.where(at_turn, got[4], jnp.where(at_end, 0.0, got[3]))
    stores = [pltpu.make_async_copy(b, a, sem.at[i]) for i, (a, b) in enumerate(bands)]
    for copy in stores:
        copy.start()
    for copy in stores:
        copy.wait()


def add_in_place(kernel, place, out, parts, scratch, sems):
    anywhere = pl.BlockSpec(memory_space=pl.ANY)
    held = pl.BlockSpec(memory_space=pltpu.HBM)
    return pl.pallas_call(
        kernel,
        out_shape=jax.ShapeDtypeStruct(out.shape, out.dtype),
        in_specs=[pl.BlockSpec(memory_space=pltpu.SMEM)] + [anywhere] * len(parts) + [held],
        out_specs=held,
        scratch_shapes=[pltpu.VMEM(shape, jnp.float32) for shape in scratch]
        + [pltpu.SemaphoreType.DMA((sems,))],
        input_output_aliases={len(parts) + 1: 0},
        cost_estimate=pl.CostEstimate(flops=10**6, bytes_accessed=6 * 10**6, transcendentals=0),
    )(place, *parts, out)


def pairs(axis, first):
    count = lax.axis_size(axis)
    lower = range(first, count - 1, 2)
    return [(i, i + 1) for i in lower] + [(i + 1, i) for i in lower]


def body(objects, probe, measurements, offsets, counts):
    row, core = lax.axis_index("row"), lax.rem(lax.axis_index("col"), 2)
    last = lax.axis_size("row") - 1
    place = jnp.stack([row, jnp.int32(last), core]).astype(jnp.int32)
    even, inner = lax.rem(row, 2) == 0, core == 0
    at_turn, at_end = (row == TURN) | (row == TURN - 1), (row == 0) | (row == last)
    turn = ((TURN - 1, TURN), (TURN, TURN - 1))
    detour = [p for p in pairs("row", 1) if p not in turn] + [(TURN - 1, 0), (TURN, last)]
    over = [(0, TURN), (last, TURN - 1)]
    far = TILE - BORDER

    def rows_of(first, x):
        return lax.ppermute(x, "row", pairs("row", first))

    def cols_of(first, x):
        return lax.ppermute(x, "col", pairs("col", first))

    def routed(x):
        got = lax.ppermute(x, "row", detour)
        return got, lax.ppermute(got, "row", over)

    def ends(x):
        low, high = x[..., :BORDER], x[..., far:]
        return jnp.where(inner, high, low), jnp.where(inner, low, high)

    low, high = objects[:, :, far:], objects[:, :, :BORDER]
    send_a, send_b = jnp.where(even, low, high), jnp.where(even, high, low)
    strip_b1, crossed = routed(send_b[1:])
    strip_b0 = rows_of(1, send_b[:1])
    strip_a = rows_of(0, send_a)
    side_a, side_b = ends(objects)
    side_b = cols_of(1, side_b)
    side_a = cols_of(0, side_a)
    shown = jnp.where(at_turn, crossed, jnp.where(at_end, 0.0, strip_b1))
    strips = jnp.concatenate([strip_a, jnp.concatenate([strip_b0, shown], axis=0)], axis=2)
    end_a, end_b = ends(strips)
    end_b = cols_of(1, end_b)
    end_a = cols_of(0, end_a)
    pieces = (objects, strip_a, strip_b0, strip_b1, crossed, side_a, side_b, end_a, end_b)
    out, strip_a, strip_b0, strip_b1, side_a, side_b, end_a, end_b = window_gradients(
        place, pieces, probe, measurements[0, 0], offsets, counts, jnp.asarray(dft_tables())
    )

    end_b = cols_of(1, end_b)
    end_a = cols_of(0, end_a)
    end_high, end_low = jnp.where(inner, end_a, end_b), jnp.where(inner, end_b, end_a)

    def folded(x, samples, part):
        held = slice(part * BORDER, (part + 1) * BORDER)
        x = x.at[..., far:].add(end_high[samples, :, held])
        return x.at[..., :BORDER].add(end_low[samples, :, held])

    strip_b1, crossed = routed(folded(strip_b1, slice(1, 2), 1))
    strip_b0 = rows_of(1, folded(strip_b0, slice(0, 1), 1))
    side_b = cols_of(1, side_b)
    strip_a = rows_of(0, folded(strip_a, slice(0, 2), 0))
    side_a = cols_of(0, side_a)
    tall, wide = (2, SAMPLES, 2, TILE, BORDER), (2, SAMPLES, 2, BORDER, TILE)
    out = add_in_place(side_kernel, place, out, (side_a, side_b), (tall, tall), 4)
    parts = (strip_a, strip_b0, strip_b1, crossed)
    return add_in_place(edge_kernel, place, out, parts, (wide, (5, 2, BORDER, TILE)), 9)


def solution(mesh):
    in_specs = (
        P(None, None, "row", "col"),
        P(),
        P("row", "col", None, None, None),
        P("row", "col", None, None),
        P("row", "col"),
    )
    out_specs = P(None, None, "row", "col")
    return jax.shard_map(body, mesh=mesh, in_specs=in_specs, out_specs=out_specs, check_vma=False)
```

```python
import functools
import math

import jax
import jax.numpy as jnp
import ml_dtypes
import numpy as np
from jax import lax
from jax.experimental import pallas as pl
from jax.experimental.pallas import tpu as pltpu
from jax.sharding import PartitionSpec as P

SAMPLES = 2
POS = 3
PROBE = 256
TILE = 512
BORDER = 128
EXT = TILE + 2 * BORDER
SMOOTHING = 0.5


HALF = PROBE // 2


def dft_tables():
    places = np.arange(HALF, dtype=np.int64)
    angle = (places[:, None] * places[None, :] % HALF) * (2.0 * math.pi / HALF)
    scale = 1.0 / math.sqrt(PROBE)
    cosines, sines = np.cos(angle) * scale, np.sin(angle) * scale
    forward = np.block([[cosines, -sines], [sines, cosines]]).astype(np.float32)
    high = forward.astype(ml_dtypes.bfloat16)
    low = (forward - high.astype(np.float32)).astype(ml_dtypes.bfloat16)
    return np.stack([high, low, high.T, low.T])


def twiddles():
    angle = np.arange(HALF) * (2.0 * math.pi / PROBE)
    lanes = [np.broadcast_to(x, (HALF, HALF)) for x in (np.cos(angle), -np.sin(angle))]
    return np.stack(lanes + [x.T for x in lanes]).astype(np.float32)


def butterfly(xr, xi, wr, wi, axis):
    (ar, br), (ai, bi) = jnp.split(xr, 2, axis), jnp.split(xi, 2, axis)
    dr, di = ar - br, ai - bi
    return (ar + br, ai + bi), (dr * wr - di * wi, dr * wi + di * wr)


def unfold(a, b, wr, wi, axis):
    (ar, ai), (br, bi) = a, b
    tr, ti = br * wr + bi * wi, bi * wr - br * wi
    return (
        jnp.concatenate([ar + tr, ar - tr], axis=axis),
        jnp.concatenate([ai + ti, ai - ti], axis=axis),
    )


def split(x):
    high = x.astype(jnp.bfloat16)
    low = (x - high.astype(jnp.float32)).astype(jnp.bfloat16)
    return high, low


def dot(a, b):
    return jnp.dot(a, b, preferred_element_type=jnp.float32)


def right_product(x, high, low):
    xh, xl = split(x)
    return dot(xh, high) + dot(xl, high) + dot(xh, low)


def left_product(high, low, x):
    xh, xl = split(x)
    return dot(high, xh) + dot(high, xl) + dot(low, xh)


FAR = BORDER + TILE
TURN = 4


def spots(place, far):
    row_a = jnp.where(lax.rem(place[0], 2) == 0, far, 0)
    col_a = jnp.where(place[2] == 0, far, 0)
    return [pl.multiple_of(v, BORDER) for v in (row_a, far - row_a, col_a, far - col_a)]


def regions(place):
    ra, rb, ca, cb = spots(place, FAR)
    return [
        (0, SAMPLES, BORDER, TILE, BORDER, TILE),
        (0, SAMPLES, ra, BORDER, BORDER, TILE),
        (0, 1, rb, BORDER, BORDER, TILE),
        (1, 1, rb, BORDER, BORDER, TILE),
        (0, SAMPLES, BORDER, TILE, ca, BORDER),
        (0, SAMPLES, BORDER, TILE, cb, BORDER),
        (0, SAMPLES, ra, BORDER, ca, BORDER),
        (0, SAMPLES, rb, BORDER, ca, BORDER),
        (0, SAMPLES, ra, BORDER, cb, BORDER),
        (0, SAMPLES, rb, BORDER, cb, BORDER),
    ]


def region_of(array, region):
    s, n, r, h, c, w = region
    return array.at[pl.ds(s, n), :, pl.ds(r, h), pl.ds(c, w)]


def halves(ref):
    return [ref.at[:, :, pl.ds(h * BORDER, BORDER)] for h in range(2)]


def turns(place):
    row = place[0]
    return (row == TURN) | (row == TURN - 1), (row == 0) | (row == place[1])


def load_pieces(place, obj, refs, sem):
    center, strip_a, strip_b0, strip_b1, crossed, side_a, side_b, end_a, end_b = refs
    sources = [center, strip_a, strip_b0, strip_b1, side_a, side_b] + halves(end_a) + halves(end_b)
    at_turn, at_end = turns(place)
    where = regions(place)
    copies = [
        pltpu.make_async_copy(src, region_of(obj, region), sem.at[i])
        for i, (src, region) in enumerate(zip(sources, where))
    ]
    for i, copy in enumerate(copies):
        if i != 3:
            copy.start()
    relayed = pltpu.make_async_copy(crossed, region_of(obj, where[3]), sem.at[3])

    @pl.when(at_turn)
    def _():
        relayed.start()

    @pl.when(jnp.logical_not(at_turn))
    def _():
        copies[3].start()

    def wait():
        for copy in copies:
            copy.wait()

        @pl.when(at_end)
        def _():
            region_of(obj, where[3])[...] = jnp.zeros((1, 2, BORDER, TILE), jnp.float32)

    return wait


def store_pieces(place, grad, refs, sem):
    center, strip_a, strip_b0, strip_b1, side_a, side_b, end_a, end_b = refs
    targets = [center, strip_a, strip_b0, strip_b1, side_a, side_b] + halves(end_a) + halves(end_b)
    copies = [
        pltpu.make_async_copy(region_of(grad, region), dst, sem.at[i])
        for i, (dst, region) in enumerate(zip(targets, regions(place)))
    ]
    for copy in copies[::-1]:
        copy.start()
    for copy in copies:
        copy.wait()


def part_kernel(measured, order, out):
    pick = order[...]
    for q in range(POS):
        x = measured[q]
        total = jnp.zeros((PROBE, PROBE), jnp.float32)
        for _ in range(3):
            piece = x.astype(jnp.bfloat16)
            x = x - piece.astype(jnp.float32)
            total += dot(dot(pick, piece).astype(jnp.bfloat16), pick.T)
        for p in range(2):
            for r in range(2):
                lanes = pl.ds((p * 2 + r) * HALF, HALF)
                out[q, :, lanes] = total[r * HALF : (r + 1) * HALF, p * HALF : (p + 1) * HALF]


def parted_measurements(measured):
    order = np.zeros((PROBE, PROBE), np.float32)
    for k in range(PROBE):
        order[k, k * 2 % PROBE + k * 2 // PROBE] = 1.0
    return pl.pallas_call(
        part_kernel,
        out_shape=jax.ShapeDtypeStruct((POS, HALF, 2 * PROBE), jnp.float32),
        cost_estimate=pl.CostEstimate(flops=10**9, bytes_accessed=10**6, transcendentals=0),
    )(measured, jnp.asarray(order.astype(ml_dtypes.bfloat16)))


def gradient_kernel(place, offsets, counts, *refs):
    ins, fixed, outs = refs[:9], refs[9:13], refs[13:21]
    obj, grad, probe, measurements, tables, twiddle, sem = refs[21:]
    samples = SAMPLES
    fixed_loads = [
        pltpu.make_async_copy(src, dst, sem.at[16 + i])
        for i, (src, dst) in enumerate(zip(fixed, (probe, measurements, tables, twiddle)))
    ]
    for copy in fixed_loads:
        copy.start()
    wait = load_pieces(place, obj, ins, sem)
    grad[...] = jnp.zeros_like(grad)
    for copy in fixed_loads:
        copy.wait()
    wait()

    lanes = lax.broadcasted_iota(jnp.int32, (PROBE, 128), 1)
    rows = lax.broadcasted_iota(jnp.int32, (8, 128), 0)

    def visit(q, carry):
        r0 = offsets[q * 2]
        c0 = offsets[q * 2 + 1]
        rt, ct = lax.rem(r0, 8), lax.rem(c0, 128)
        ra = pl.multiple_of(r0 - rt, 8)
        rz = pl.multiple_of(jnp.minimum(ra + PROBE, EXT - 8), 8)
        ca = pl.multiple_of(c0 - ct, 128)
        cb = pl.multiple_of(ca + 128, 128)
        cz = pl.multiple_of(jnp.minimum(ca + 256, EXT - 128), 128)
        early = lanes < ct
        above = rows < rt

        pr = pltpu.roll(pltpu.roll(probe[0], rt, 0), ct, 1)
        pi = pltpu.roll(pltpu.roll(probe[1], rt, 0), ct, 1)

        def block(s, k, col):
            head = jnp.where(
                above,
                obj[s, k, pl.ds(rz, 8), pl.ds(col, 128)],
                obj[s, k, pl.ds(ra, 8), pl.ds(col, 128)],
            )
            tail = obj[s, k, pl.ds(pl.multiple_of(ra + 8, 8), PROBE - 8), pl.ds(col, 128)]
            return jnp.concatenate([head, tail], axis=0)

        def frame(s, k):
            first = jnp.where(early, block(s, k, cz), block(s, k, ca))
            return jnp.concatenate([first, block(s, k, cb)], axis=1)

        def scatter(s, k, value):
            def add(col, v):
                grad[s, k, pl.ds(pl.multiple_of(ra + 8, 8), PROBE - 8), pl.ds(col, 128)] += v[8:]
                grad[s, k, pl.ds(ra, 8), pl.ds(col, 128)] += jnp.where(above, 0.0, v[:8])
                grad[s, k, pl.ds(rz, 8), pl.ds(col, 128)] += jnp.where(above, v[:8], 0.0)

            first = value[:, :128]
            add(ca, jnp.where(early, 0.0, first))
            add(cz, jnp.where(early, first, 0.0))
            add(cb, value[:, 128:])

        lane_r, lane_i = twiddle[0, 0:1], twiddle[1, 0:1]
        row_r, row_i = twiddle[2], twiddle[3]
        waves = []
        for s in range(samples):
            o_r, o_i = frame(s, 0), frame(s, 1)
            waves.append((pr * o_r - pi * o_i, pr * o_i + pi * o_r))
        parts = [butterfly(*wave, lane_r, lane_i, 1) for wave in waves]
        stacked = [
            jnp.concatenate(parts[s][p], axis=1) for p in range(2) for s in range(samples)
        ]
        half = right_product(jnp.concatenate(stacked, axis=0), tables[0], tables[1])
        blocks = []
        for s in range(samples):
            for p in range(2):
                y = half[(p * samples + s) * PROBE : (p * samples + s + 1) * PROBE]
                for pair in butterfly(y[:, :HALF], y[:, HALF:], row_r, row_i, 0):
                    blocks.append(jnp.concatenate(pair, axis=0))
        spectrum = left_product(tables[2], tables[3], jnp.concatenate(blocks, axis=1))
        s_r, s_i = spectrum[:HALF], spectrum[HALF:]
        m = jnp.concatenate([measurements[q]] * samples, axis=1)
        factor = 1.0 - m * lax.rsqrt(s_r * s_r + s_i * s_i + SMOOTHING)
        scaled = jnp.concatenate([s_r * factor, s_i * factor], axis=0)
        back = left_product(tables[0], tables[1], scaled)
        stacked = []
        for p in range(2):
            for s in range(samples):
                at = (s * 2 + p) * PROBE
                a, b = back[:, at : at + HALF], back[:, at + HALF : at + PROBE]
                pair = unfold((a[:HALF], a[HALF:]), (b[:HALF], b[HALF:]), row_r, row_i, 0)
                stacked.append(jnp.concatenate(pair, axis=1))
        final = right_product(jnp.concatenate(stacked, axis=0), tables[2], tables[3])
        for s in range(samples):
            a = final[s * PROBE : (s + 1) * PROBE]
            b = final[(samples + s) * PROBE : (samples + s + 1) * PROBE]
            b_r, b_i = unfold(
                (a[:, :HALF], a[:, HALF:]), (b[:, :HALF], b[:, HALF:]), lane_r, lane_i, 1
            )
            scatter(s, 0, pr * b_r + pi * b_i)
            scatter(s, 1, pr * b_i - pi * b_r)
        return carry

    lax.fori_loop(0, counts[0], visit, 0)
    store_pieces(place, grad, outs, sem)


def window_gradients(place, pieces, probe, measurements, offsets, counts, tables):
    def shape(*dims):
        return jax.ShapeDtypeStruct(dims, jnp.float32)

    strip, side = shape(1, 2, BORDER, TILE), shape(SAMPLES, 2, TILE, BORDER)
    end = shape(SAMPLES, 2, 2 * BORDER, BORDER)
    shapes = [shape(SAMPLES, 2, TILE, TILE), shape(SAMPLES, 2, BORDER, TILE)]
    shapes += [strip] * 2 + [side] * 2 + [end] * 2
    anywhere = pl.BlockSpec(memory_space=pl.ANY)
    scalars = pl.BlockSpec(memory_space=pltpu.SMEM)
    return pl.pallas_call(
        gradient_kernel,
        out_shape=shapes,
        in_specs=[scalars] * 3 + [anywhere] * (len(pieces) + 4),
        out_specs=[pl.BlockSpec(memory_space=pltpu.HBM)] + [anywhere] * 7,
        scratch_shapes=[
            pltpu.VMEM((SAMPLES, 2, EXT, EXT), jnp.float32),
            pltpu.VMEM((SAMPLES, 2, EXT, EXT), jnp.float32),
            pltpu.VMEM((2, PROBE, PROBE), jnp.float32),
            pltpu.VMEM((POS, HALF, 2 * PROBE), jnp.float32),
            pltpu.VMEM((4, PROBE, PROBE), jnp.bfloat16),
            pltpu.VMEM((4, HALF, HALF), jnp.float32),
            pltpu.SemaphoreType.DMA((20,)),
        ],
        compiler_params=pltpu.CompilerParams(vmem_limit_bytes=48 * 1024 * 1024),
        cost_estimate=pl.CostEstimate(flops=10**10, bytes_accessed=3 * 10**7, transcendentals=0),
    )(place, offsets.reshape(-1), counts.reshape(-1), *pieces, probe, measurements, *tables)


def side_kernel(place, side_a, side_b, held, out, band, got, sem):
    starts = spots(place, TILE - BORDER)[2:]
    loads = []
    for e, (src, first) in enumerate(zip((side_a, side_b), starts)):
        loads.append((out.at[:, :, :, pl.ds(first, BORDER)], band.at[e]))
        loads.append((src, got.at[e]))
    loads = [pltpu.make_async_copy(a, b, sem.at[i]) for i, (a, b) in enumerate(loads)]
    for copy in loads:
        copy.start()
    for copy in loads:
        copy.wait()
    band[...] += got[...]
    stores = [
        pltpu.make_async_copy(band.at[e], out.at[:, :, :, pl.ds(first, BORDER)], sem.at[e])
        for e, first in enumerate(starts)
    ]
    for copy in stores:
        copy.start()
    for copy in stores:
        copy.wait()


def edge_kernel(place, strip_a, strip_b0, strip_b1, crossed, held, out, band, got, sem):
    starts = spots(place, TILE - BORDER)[:2]
    at_turn, at_end = turns(place)
    bands = [
        (out.at[s, :, pl.ds(first, BORDER)], band.at[e, s])
        for e, first in enumerate(starts)
        for s in range(SAMPLES)
    ]
    strips = (strip_a.at[0], strip_a.at[1], strip_b0.at[0], strip_b1.at[0], crossed.at[0])
    count = len(bands)
    early = [pltpu.make_async_copy(a, b, sem.at[i]) for i, (a, b) in enumerate(bands)]
    late = [
        pltpu.make_async_copy(src, got.at[i], sem.at[count + i]) for i, src in enumerate(strips)
    ]
    for i in range(count):
        early[i].start()
        late[i].start()
    late[count].start()
    stores = []
    for i, (a, b) in enumerate(bands):
        early[i].wait()
        late[i].wait()
        if i < count - 1:
            b[...] += got[i]
        else:
            late[count].wait()
            b[...] += jnp.where(at_turn, got[count], jnp.where(at_end, 0.0, got[i]))
        stores.append(pltpu.make_async_copy(b, a, sem.at[i]))
        stores[-1].start()
    for copy in stores:
        copy.wait()


def add_in_place(kernel, place, out, parts, scratch, sems):
    anywhere = pl.BlockSpec(memory_space=pl.ANY)
    held = pl.BlockSpec(memory_space=pltpu.HBM)
    return pl.pallas_call(
        kernel,
        out_shape=jax.ShapeDtypeStruct(out.shape, out.dtype),
        in_specs=[pl.BlockSpec(memory_space=pltpu.SMEM)] + [anywhere] * len(parts) + [held],
        out_specs=held,
        scratch_shapes=[pltpu.VMEM(shape, jnp.float32) for shape in scratch]
        + [pltpu.SemaphoreType.DMA((sems,))],
        input_output_aliases={len(parts) + 1: 0},
        cost_estimate=pl.CostEstimate(flops=10**6, bytes_accessed=6 * 10**6, transcendentals=0),
    )(place, *parts, out)


def pairs(axis, first):
    count = lax.axis_size(axis)
    lower = range(first, count - 1, 2)
    return [(i, i + 1) for i in lower] + [(i + 1, i) for i in lower]


def body(objects, probe, measurements, offsets, counts):
    row, core = lax.axis_index("row"), lax.rem(lax.axis_index("col"), 2)
    last = lax.axis_size("row") - 1
    place = jnp.stack([row, jnp.int32(last), core]).astype(jnp.int32)
    even, inner = lax.rem(row, 2) == 0, core == 0
    at_turn, at_end = (row == TURN) | (row == TURN - 1), (row == 0) | (row == last)
    turn = ((TURN - 1, TURN), (TURN, TURN - 1))
    detour = [p for p in pairs("row", 1) if p not in turn] + [(TURN - 1, 0), (TURN, last)]
    over = [(0, TURN), (last, TURN - 1)]
    far = TILE - BORDER

    def rows_of(first, x):
        return lax.ppermute(x, "row", pairs("row", first))

    def cols_of(first, x):
        return lax.ppermute(x, "col", pairs("col", first))

    def routed(x, *others):
        got, *others = lax.optimization_barrier((lax.ppermute(x, "row", detour), *others))
        return got, lax.ppermute(got, "row", over), *others

    def ends(x):
        low, high = x[..., :BORDER], x[..., far:]
        return jnp.where(inner, high, low), jnp.where(inner, low, high)

    low, high = objects[:, :, far:], objects[:, :, :BORDER]
    send_a, send_b = jnp.where(even, low, high), jnp.where(even, high, low)
    side_a, side_b = ends(objects)
    strip_b1, crossed, side_b = routed(send_b[1:], cols_of(1, side_b))
    strip_b0 = rows_of(1, send_b[:1])
    strip_a = rows_of(0, send_a)
    side_a = cols_of(0, side_a)
    shown = jnp.where(at_turn, crossed, jnp.where(at_end, 0.0, strip_b1))
    strips = jnp.concatenate([strip_a, jnp.concatenate([strip_b0, shown], axis=0)], axis=2)
    end_a, end_b = ends(strips)
    end_b = cols_of(1, end_b)
    end_a = cols_of(0, end_a)
    parted = parted_measurements(measurements[0, 0])
    pieces = (objects, strip_a, strip_b0, strip_b1, crossed, side_a, side_b, end_a, end_b)
    out, strip_a, strip_b0, strip_b1, side_a, side_b, end_a, end_b = window_gradients(
        place, pieces, probe, parted, offsets, counts, [jnp.asarray(dft_tables()), jnp.asarray(twiddles())]
    )

    end_b = cols_of(1, end_b)
    end_a = cols_of(0, end_a)
    end_high, end_low = jnp.where(inner, end_a, end_b), jnp.where(inner, end_b, end_a)

    def folded(x, samples, part):
        held = slice(part * BORDER, (part + 1) * BORDER)
        x = x.at[..., far:].add(end_high[samples, :, held])
        return x.at[..., :BORDER].add(end_low[samples, :, held])

    strip_b1, crossed = routed(folded(strip_b1, slice(1, 2), 1))
    strip_b0 = rows_of(1, folded(strip_b0, slice(0, 1), 1))
    side_b = cols_of(1, side_b)
    strip_a = rows_of(0, folded(strip_a, slice(0, 2), 0))
    side_a = cols_of(0, side_a)
    tall, wide = (2, SAMPLES, 2, TILE, BORDER), (2, SAMPLES, 2, BORDER, TILE)
    out = add_in_place(side_kernel, place, out, (side_a, side_b), (tall, tall), 4)
    parts = (strip_a, strip_b0, strip_b1, crossed)
    return add_in_place(edge_kernel, place, out, parts, (wide, (5, 2, BORDER, TILE)), 9)


def solution(mesh):
    in_specs = (
        P(None, None, "row", "col"),
        P(),
        P("row", "col", None, None, None),
        P("row", "col", None, None),
        P("row", "col"),
    )
    out_specs = P(None, None, "row", "col")
    return jax.shard_map(body, mesh=mesh, in_specs=in_specs, out_specs=out_specs, check_vma=False)
```

```python
import functools
import math

import jax
import jax.numpy as jnp
import ml_dtypes
import numpy as np
from jax import lax
from jax.experimental import pallas as pl
from jax.experimental.pallas import tpu as pltpu
from jax.sharding import PartitionSpec as P

SAMPLES = 2
POS = 3
PROBE = 256
TILE = 512
BORDER = 128
EXT = TILE + 2 * BORDER
SMOOTHING = 0.5


HALF = PROBE // 2


def dft_tables():
    places = np.arange(HALF, dtype=np.int64)
    angle = (places[:, None] * places[None, :] % HALF) * (2.0 * math.pi / HALF)
    scale = 1.0 / math.sqrt(PROBE)
    cosines, sines = np.cos(angle) * scale, np.sin(angle) * scale
    forward = np.block([[cosines, -sines], [sines, cosines]]).astype(np.float32)
    high = forward.astype(ml_dtypes.bfloat16)
    low = (forward - high.astype(np.float32)).astype(ml_dtypes.bfloat16)
    return np.stack([high, low, high.T, low.T])


def twiddles():
    angle = np.arange(HALF) * (2.0 * math.pi / PROBE)
    lanes = [np.broadcast_to(x, (HALF, HALF)) for x in (np.cos(angle), -np.sin(angle))]
    return np.stack(lanes + [x.T for x in lanes]).astype(np.float32)


def butterfly(xr, xi, wr, wi, axis):
    (ar, br), (ai, bi) = jnp.split(xr, 2, axis), jnp.split(xi, 2, axis)
    dr, di = ar - br, ai - bi
    return (ar + br, ai + bi), (dr * wr - di * wi, dr * wi + di * wr)


def unfold(a, b, wr, wi, axis):
    (ar, ai), (br, bi) = a, b
    tr, ti = br * wr + bi * wi, bi * wr - br * wi
    return (
        jnp.concatenate([ar + tr, ar - tr], axis=axis),
        jnp.concatenate([ai + ti, ai - ti], axis=axis),
    )


def split(x):
    high = x.astype(jnp.bfloat16)
    low = (x - high.astype(jnp.float32)).astype(jnp.bfloat16)
    return high, low


def dot(a, b):
    return jnp.dot(a, b, preferred_element_type=jnp.float32)


def right_product(x, high, low):
    xh, xl = split(x)
    return dot(xh, high) + dot(xl, high) + dot(xh, low)


def left_product(high, low, x):
    xh, xl = split(x)
    return dot(high, xh) + dot(high, xl) + dot(low, xh)


FAR = BORDER + TILE
TURN = 4


def spots(place, far):
    row_a = jnp.where(lax.rem(place[0], 2) == 0, far, 0)
    col_a = jnp.where(place[2] == 0, far, 0)
    return [pl.multiple_of(v, BORDER) for v in (row_a, far - row_a, col_a, far - col_a)]


def regions(place):
    ra, rb, ca, cb = spots(place, FAR)
    return [
        (0, SAMPLES, BORDER, TILE, BORDER, TILE),
        (0, SAMPLES, ra, BORDER, BORDER, TILE),
        (0, 1, rb, BORDER, BORDER, TILE),
        (1, 1, rb, BORDER, BORDER, TILE),
        (0, SAMPLES, BORDER, TILE, ca, BORDER),
        (0, SAMPLES, BORDER, TILE, cb, BORDER),
        (0, SAMPLES, ra, BORDER, ca, BORDER),
        (0, SAMPLES, rb, BORDER, ca, BORDER),
        (0, SAMPLES, ra, BORDER, cb, BORDER),
        (0, SAMPLES, rb, BORDER, cb, BORDER),
    ]


def region_of(array, region):
    s, n, r, h, c, w = region
    return array.at[pl.ds(s, n), :, pl.ds(r, h), pl.ds(c, w)]


def halves(ref):
    return [ref.at[:, :, pl.ds(h * BORDER, BORDER)] for h in range(2)]


def turns(place):
    row = place[0]
    return (row == TURN) | (row == TURN - 1), (row == 0) | (row == place[1])


def load_pieces(place, obj, refs, sem):
    center, strip_a, strip_b0, strip_b1, crossed, side_a, side_b, end_a, end_b = refs
    sources = [center, strip_a, strip_b0, strip_b1, side_a, side_b] + halves(end_a) + halves(end_b)
    at_turn, at_end = turns(place)
    where = regions(place)
    copies = [
        pltpu.make_async_copy(src, region_of(obj, region), sem.at[i])
        for i, (src, region) in enumerate(zip(sources, where))
    ]
    for i, copy in enumerate(copies):
        if i != 3:
            copy.start()
    relayed = pltpu.make_async_copy(crossed, region_of(obj, where[3]), sem.at[3])

    @pl.when(at_turn)
    def _():
        relayed.start()

    @pl.when(jnp.logical_not(at_turn))
    def _():
        copies[3].start()

    def wait():
        for copy in copies:
            copy.wait()

        @pl.when(at_end)
        def _():
            region_of(obj, where[3])[...] = jnp.zeros((1, 2, BORDER, TILE), jnp.float32)

    return wait


def store_pieces(place, grad, refs, sem):
    center, strip_a, strip_b0, strip_b1, side_a, side_b, end_a, end_b = refs
    targets = [center, strip_a, strip_b0, strip_b1, side_a, side_b] + halves(end_a) + halves(end_b)
    copies = [
        pltpu.make_async_copy(region_of(grad, region), dst, sem.at[i])
        for i, (dst, region) in enumerate(zip(targets, regions(place)))
    ]
    for copy in copies[::-1]:
        copy.start()
    for copy in copies:
        copy.wait()


def part_kernel(measured, order, out):
    pick = order[...]
    for q in range(POS):
        x = measured[q]
        total = jnp.zeros((PROBE, PROBE), jnp.float32)
        for _ in range(3):
            piece = x.astype(jnp.bfloat16)
            x = x - piece.astype(jnp.float32)
            total += dot(dot(pick, piece).astype(jnp.bfloat16), pick.T)
        for p in range(2):
            for r in range(2):
                lanes = pl.ds((p * 2 + r) * HALF, HALF)
                out[q, :, lanes] = total[r * HALF : (r + 1) * HALF, p * HALF : (p + 1) * HALF]


def parted_measurements(measured):
    order = np.zeros((PROBE, PROBE), np.float32)
    for k in range(PROBE):
        order[k, k * 2 % PROBE + k * 2 // PROBE] = 1.0
    return pl.pallas_call(
        part_kernel,
        out_shape=jax.ShapeDtypeStruct((POS, HALF, 2 * PROBE), jnp.float32),
        cost_estimate=pl.CostEstimate(flops=10**9, bytes_accessed=10**6, transcendentals=0),
    )(measured, jnp.asarray(order.astype(ml_dtypes.bfloat16)))


def gradient_kernel(place, offsets, counts, *refs):
    ins, fixed, outs = refs[:9], refs[9:13], refs[13:21]
    obj, grad, probe, measurements, tables, twiddle, sem = refs[21:]
    samples = SAMPLES
    fixed_loads = [
        pltpu.make_async_copy(src, dst, sem.at[16 + i])
        for i, (src, dst) in enumerate(zip(fixed, (probe, measurements, tables, twiddle)))
    ]
    for copy in fixed_loads:
        copy.start()
    wait = load_pieces(place, obj, ins, sem)
    grad[...] = jnp.zeros_like(grad)
    for copy in fixed_loads:
        copy.wait()
    wait()

    lanes = lax.broadcasted_iota(jnp.int32, (PROBE, 128), 1)
    rows = lax.broadcasted_iota(jnp.int32, (8, 128), 0)

    def visit(q, carry):
        r0 = offsets[q * 2]
        c0 = offsets[q * 2 + 1]
        rt, ct = lax.rem(r0, 8), lax.rem(c0, 128)
        ra = pl.multiple_of(r0 - rt, 8)
        rz = pl.multiple_of(jnp.minimum(ra + PROBE, EXT - 8), 8)
        ca = pl.multiple_of(c0 - ct, 128)
        cb = pl.multiple_of(ca + 128, 128)
        cz = pl.multiple_of(jnp.minimum(ca + 256, EXT - 128), 128)
        early = lanes < ct
        above = rows < rt

        pr = pltpu.roll(pltpu.roll(probe[0], rt, 0), ct, 1)
        pi = pltpu.roll(pltpu.roll(probe[1], rt, 0), ct, 1)

        def block(s, k, col):
            head = jnp.where(
                above,
                obj[s, k, pl.ds(rz, 8), pl.ds(col, 128)],
                obj[s, k, pl.ds(ra, 8), pl.ds(col, 128)],
            )
            tail = obj[s, k, pl.ds(pl.multiple_of(ra + 8, 8), PROBE - 8), pl.ds(col, 128)]
            return jnp.concatenate([head, tail], axis=0)

        def frame(s, k):
            first = jnp.where(early, block(s, k, cz), block(s, k, ca))
            return jnp.concatenate([first, block(s, k, cb)], axis=1)

        def scatter(s, k, value):
            def add(col, v):
                grad[s, k, pl.ds(pl.multiple_of(ra + 8, 8), PROBE - 8), pl.ds(col, 128)] += v[8:]
                grad[s, k, pl.ds(ra, 8), pl.ds(col, 128)] += jnp.where(above, 0.0, v[:8])
                grad[s, k, pl.ds(rz, 8), pl.ds(col, 128)] += jnp.where(above, v[:8], 0.0)

            first = value[:, :128]
            add(ca, jnp.where(early, 0.0, first))
            add(cz, jnp.where(early, first, 0.0))
            add(cb, value[:, 128:])

        lane_r, lane_i = twiddle[0, 0:1], twiddle[1, 0:1]
        row_r, row_i = twiddle[2], twiddle[3]
        waves = []
        for s in range(samples):
            o_r, o_i = frame(s, 0), frame(s, 1)
            waves.append((pr * o_r - pi * o_i, pr * o_i + pi * o_r))
        parts = [butterfly(*wave, lane_r, lane_i, 1) for wave in waves]
        stacked = [
            jnp.concatenate(parts[s][p], axis=1) for p in range(2) for s in range(samples)
        ]
        half = right_product(jnp.concatenate(stacked, axis=0), tables[0], tables[1])
        blocks = []
        for s in range(samples):
            for p in range(2):
                y = half[(p * samples + s) * PROBE : (p * samples + s + 1) * PROBE]
                for pair in butterfly(y[:, :HALF], y[:, HALF:], row_r, row_i, 0):
                    blocks.append(jnp.concatenate(pair, axis=0))
        spectrum = left_product(tables[2], tables[3], jnp.concatenate(blocks, axis=1))
        s_r, s_i = spectrum[:HALF], spectrum[HALF:]
        m = jnp.concatenate([measurements[q]] * samples, axis=1)
        factor = 1.0 - m * lax.rsqrt(s_r * s_r + s_i * s_i + SMOOTHING)
        scaled = jnp.concatenate([s_r * factor, s_i * factor], axis=0)
        back = left_product(tables[0], tables[1], scaled)
        stacked = []
        for p in range(2):
            for s in range(samples):
                at = (s * 2 + p) * PROBE
                a, b = back[:, at : at + HALF], back[:, at + HALF : at + PROBE]
                pair = unfold((a[:HALF], a[HALF:]), (b[:HALF], b[HALF:]), row_r, row_i, 0)
                stacked.append(jnp.concatenate(pair, axis=1))
        final = right_product(jnp.concatenate(stacked, axis=0), tables[2], tables[3])
        for s in range(samples):
            a = final[s * PROBE : (s + 1) * PROBE]
            b = final[(samples + s) * PROBE : (samples + s + 1) * PROBE]
            b_r, b_i = unfold(
                (a[:, :HALF], a[:, HALF:]), (b[:, :HALF], b[:, HALF:]), lane_r, lane_i, 1
            )
            scatter(s, 0, pr * b_r + pi * b_i)
            scatter(s, 1, pr * b_i - pi * b_r)
        return carry

    lax.fori_loop(0, counts[0], visit, 0)
    store_pieces(place, grad, outs, sem)


def window_gradients(place, pieces, probe, measurements, offsets, counts, tables):
    def shape(*dims):
        return jax.ShapeDtypeStruct(dims, jnp.float32)

    strip, side = shape(1, 2, BORDER, TILE), shape(SAMPLES, 2, TILE, BORDER)
    end = shape(SAMPLES, 2, 2 * BORDER, BORDER)
    shapes = [shape(SAMPLES, 2, TILE, TILE), shape(SAMPLES, 2, BORDER, TILE)]
    shapes += [strip] * 2 + [side] * 2 + [end] * 2
    anywhere = pl.BlockSpec(memory_space=pl.ANY)
    scalars = pl.BlockSpec(memory_space=pltpu.SMEM)
    return pl.pallas_call(
        gradient_kernel,
        out_shape=shapes,
        in_specs=[scalars] * 3 + [anywhere] * (len(pieces) + 4),
        out_specs=[pl.BlockSpec(memory_space=pltpu.HBM)] + [anywhere] * 7,
        scratch_shapes=[
            pltpu.VMEM((SAMPLES, 2, EXT, EXT), jnp.float32),
            pltpu.VMEM((SAMPLES, 2, EXT, EXT), jnp.float32),
            pltpu.VMEM((2, PROBE, PROBE), jnp.float32),
            pltpu.VMEM((POS, HALF, 2 * PROBE), jnp.float32),
            pltpu.VMEM((4, PROBE, PROBE), jnp.bfloat16),
            pltpu.VMEM((4, HALF, HALF), jnp.float32),
            pltpu.SemaphoreType.DMA((20,)),
        ],
        compiler_params=pltpu.CompilerParams(vmem_limit_bytes=58 * 1024 * 1024),
        cost_estimate=pl.CostEstimate(flops=10**10, bytes_accessed=3 * 10**7, transcendentals=0),
    )(place, offsets.reshape(-1), counts.reshape(-1), *pieces, probe, measurements, *tables)


def side_kernel(place, side_a, side_b, held, out, band, got, sem):
    starts = spots(place, TILE - BORDER)[2:]
    loads = []
    for e, (src, first) in enumerate(zip((side_a, side_b), starts)):
        loads.append((out.at[:, :, :, pl.ds(first, BORDER)], band.at[e]))
        loads.append((src, got.at[e]))
    loads = [pltpu.make_async_copy(a, b, sem.at[i]) for i, (a, b) in enumerate(loads)]
    for copy in loads:
        copy.start()
    for copy in loads:
        copy.wait()
    band[...] += got[...]
    stores = [
        pltpu.make_async_copy(band.at[e], out.at[:, :, :, pl.ds(first, BORDER)], sem.at[e])
        for e, first in enumerate(starts)
    ]
    for copy in stores:
        copy.start()
    for copy in stores:
        copy.wait()


def edge_kernel(place, strip_a, strip_b0, strip_b1, crossed, held, out, band, got, sem):
    starts = spots(place, TILE - BORDER)[:2]
    at_turn, at_end = turns(place)
    bands = [
        (out.at[s, :, pl.ds(first, BORDER)], band.at[e, s])
        for e, first in enumerate(starts)
        for s in range(SAMPLES)
    ]
    strips = (strip_a.at[0], strip_a.at[1], strip_b0.at[0], strip_b1.at[0], crossed.at[0])
    count = len(bands)
    early = [pltpu.make_async_copy(a, b, sem.at[i]) for i, (a, b) in enumerate(bands)]
    late = [
        pltpu.make_async_copy(src, got.at[i], sem.at[count + i]) for i, src in enumerate(strips)
    ]
    for i in range(count):
        early[i].start()
        late[i].start()
    late[count].start()
    stores = []
    for i, (a, b) in enumerate(bands):
        early[i].wait()
        late[i].wait()
        if i < count - 1:
            b[...] += got[i]
        else:
            late[count].wait()
            b[...] += jnp.where(at_turn, got[count], jnp.where(at_end, 0.0, got[i]))
        stores.append(pltpu.make_async_copy(b, a, sem.at[i]))
        stores[-1].start()
    for copy in stores:
        copy.wait()


def add_in_place(kernel, place, out, parts, scratch, sems):
    anywhere = pl.BlockSpec(memory_space=pl.ANY)
    held = pl.BlockSpec(memory_space=pltpu.HBM)
    return pl.pallas_call(
        kernel,
        out_shape=jax.ShapeDtypeStruct(out.shape, out.dtype),
        in_specs=[pl.BlockSpec(memory_space=pltpu.SMEM)] + [anywhere] * len(parts) + [held],
        out_specs=held,
        scratch_shapes=[pltpu.VMEM(shape, jnp.float32) for shape in scratch]
        + [pltpu.SemaphoreType.DMA((sems,))],
        input_output_aliases={len(parts) + 1: 0},
        cost_estimate=pl.CostEstimate(flops=10**6, bytes_accessed=6 * 10**6, transcendentals=0),
    )(place, *parts, out)


def pairs(axis, first):
    count = lax.axis_size(axis)
    lower = range(first, count - 1, 2)
    return [(i, i + 1) for i in lower] + [(i + 1, i) for i in lower]


def body(objects, probe, measurements, offsets, counts):
    row, core = lax.axis_index("row"), lax.rem(lax.axis_index("col"), 2)
    last = lax.axis_size("row") - 1
    place = jnp.stack([row, jnp.int32(last), core]).astype(jnp.int32)
    even, inner = lax.rem(row, 2) == 0, core == 0
    at_turn, at_end = (row == TURN) | (row == TURN - 1), (row == 0) | (row == last)
    turn = ((TURN - 1, TURN), (TURN, TURN - 1))
    detour = [p for p in pairs("row", 1) if p not in turn] + [(TURN - 1, 0), (TURN, last)]
    over = [(0, TURN), (last, TURN - 1)]
    far = TILE - BORDER

    def rows_of(first, x):
        return lax.ppermute(x, "row", pairs("row", first))

    def cols_of(first, x):
        return lax.ppermute(x, "col", pairs("col", first))

    def routed(x, *others):
        got, *others = lax.optimization_barrier((lax.ppermute(x, "row", detour), *others))
        return got, lax.ppermute(got, "row", over), *others

    def ends(x):
        low, high = x[..., :BORDER], x[..., far:]
        return jnp.where(inner, high, low), jnp.where(inner, low, high)

    low, high = objects[:, :, far:], objects[:, :, :BORDER]
    send_a, send_b = jnp.where(even, low, high), jnp.where(even, high, low)
    side_a, side_b = ends(objects)
    strip_b1, crossed, side_b = routed(send_b[1:], cols_of(1, side_b))
    strip_b0 = rows_of(1, send_b[:1])
    strip_a = rows_of(0, send_a)
    side_a = cols_of(0, side_a)
    shown = jnp.where(at_turn, crossed, jnp.where(at_end, 0.0, strip_b1))
    strips = jnp.concatenate([strip_a, jnp.concatenate([strip_b0, shown], axis=0)], axis=2)
    end_a, end_b = ends(strips)
    end_b = cols_of(1, end_b)
    end_a = cols_of(0, end_a)
    parted = parted_measurements(measurements[0, 0])
    pieces = (objects, strip_a, strip_b0, strip_b1, crossed, side_a, side_b, end_a, end_b)
    out, strip_a, strip_b0, strip_b1, side_a, side_b, end_a, end_b = window_gradients(
        place, pieces, probe, parted, offsets, counts, [jnp.asarray(dft_tables()), jnp.asarray(twiddles())]
    )

    end_b = cols_of(1, end_b)
    end_a = cols_of(0, end_a)
    end_high, end_low = jnp.where(inner, end_a, end_b), jnp.where(inner, end_b, end_a)

    def folded(x, samples, part):
        held = slice(part * BORDER, (part + 1) * BORDER)
        x = x.at[..., far:].add(end_high[samples, :, held])
        return x.at[..., :BORDER].add(end_low[samples, :, held])

    strip_b1, crossed = routed(folded(strip_b1, slice(1, 2), 1))
    strip_b0 = rows_of(1, folded(strip_b0, slice(0, 1), 1))
    side_b = cols_of(1, side_b)
    strip_a = rows_of(0, folded(strip_a, slice(0, 2), 0))
    side_a = cols_of(0, side_a)
    tall, wide = (2, SAMPLES, 2, TILE, BORDER), (2, SAMPLES, 2, BORDER, TILE)
    out = add_in_place(side_kernel, place, out, (side_a, side_b), (tall, tall), 4)
    parts = (strip_a, strip_b0, strip_b1, crossed)
    return add_in_place(edge_kernel, place, out, parts, (wide, (5, 2, BORDER, TILE)), 9)


def solution(mesh):
    in_specs = (
        P(None, None, "row", "col"),
        P(),
        P("row", "col", None, None, None),
        P("row", "col", None, None),
        P("row", "col"),
    )
    out_specs = P(None, None, "row", "col")
    return jax.shard_map(body, mesh=mesh, in_specs=in_specs, out_specs=out_specs, check_vma=False)
```
